256 devices in a mesh: subj: 8 (over y, core), vox: 32 (over z, x).
Axes of the slice: x: 4, y: 4, z: 8, core: 2. Of those that a mesh axis runs over, the one named last changes fastest.
Arguments:
- scans: bfloat16 [16, 65536, 1024], P('subj', 'vox'), may hold values from -48 to 48
- start_maps: bfloat16 [16, 64, 65536], P('subj', None, 'vox'), may hold values from -6 to 6
Outputs:
- shared_resp: float32 [64, 1024], P(None, 'vox')
- subject_maps: bfloat16 [16, 64, 65536], P('subj', None, 'vox')
The draws below stay inside these ranges and needn't reach their ends.
All inputs are finite; a program needn't handle non-finite values.
Results may differ from the reference program's by a relative error of at most 0.011.
Values may be sent and summed in bfloat16 or wider, within the bound.
No kernel may reach another device: no remote copies, remote signals or barrier semaphores. Data moves between devices by JAX's collectives and lax.ppermute only.
A program may use at most 64 MiB of HBM per device.

```python
import math
import jax
import jax.numpy as jnp
from jax import lax

FEATURES = 64
FRAMES = 1024
ITERS = 6
SUBJECTS = 16
VOXELS = 65536


def draw_scans(key, part):
    keys = jax.random.split(key, 3)
    rise = 3.0 ** (jnp.arange(VOXELS, dtype=jnp.float32) / VOXELS)
    jitter = 10.0 ** jax.random.uniform(keys[0], (VOXELS,), jnp.float32)
    row_scale = 0.2 * rise * jitter
    col_scale = 2.0 ** jax.random.uniform(keys[1], (FRAMES,), jnp.float32, -1.0, 1.0)
    values = jax.random.truncated_normal(keys[2], -4.0, 4.0, (SUBJECTS, VOXELS, FRAMES), jnp.float32)
    return (values * row_scale[None, :, None] * col_scale[None, None, :]).astype(jnp.bfloat16)


def block_levels(own_key, dims, cuts, least, high):
    def one(position, shards_of):
        heights = jax.random.uniform(jax.random.fold_in(jax.random.fold_in(own_key, 6), position), (shards_of,), jnp.float32, least / len(cuts), high / len(cuts))
        return jnp.repeat(jnp.exp(heights), dims[position] // shards_of).reshape((-1,) + (1,) * (len(dims) - position - 1))

    level = one(*cuts[0])
    for cut in cuts[1:]:
        level = level * one(*cut)
    return level


def scatter_about(rng, extent, spread, reach, pieces=(), held_as=jnp.bfloat16):
    result = spread * jax.random.normal(rng, extent, jnp.float32)
    if pieces:
        result = result * block_levels(rng, extent, pieces, -0.22, 0.18)
    return jnp.clip(result, -reach, reach).astype(held_as)


def setup_inputs(seed: int = 0) -> dict:
    key_list = jax.random.split(jax.random.key(seed), 3)
    scans = draw_scans(jax.random.fold_in(key_list[2], 71), 0)
    start_maps = scatter_about(key_list[1], (SUBJECTS, FEATURES, VOXELS), 1.0, 6.0, ((0, 8), (2, 32)))
    return {"scans": scans, "start_maps": start_maps}


def polar_factor(projection_target):
    newton_iterate = projection_target / jnp.sqrt(jnp.sum(projection_target * projection_target))
    identity = jnp.eye(projection_target.shape[0], dtype=jnp.float32)
    for step in range(ITERS):
        gram = jnp.dot(newton_iterate, newton_iterate.T, precision=lax.Precision.HIGHEST)
        newton_iterate = jnp.dot(1.5 * identity - 0.5 * gram, newton_iterate, precision=lax.Precision.HIGHEST)
    return newton_iterate

def update(subject_projections, scans):
    partials = lax.map(lambda pair: jnp.dot(pair[0], pair[1], preferred_element_type=jnp.float32), (subject_projections, scans))
    shared = lax.optimization_barrier(jnp.sum(partials, axis=0)) / (SUBJECTS * math.sqrt(VOXELS))
    shared_response_second = shared.astype(jnp.bfloat16)

    def fit_subject(series):
        projection_target = lax.dot_general(shared_response_second, series, (((1,), (1,)), ((), ())), preferred_element_type=jnp.float32)
        return (polar_factor(projection_target) * math.sqrt(VOXELS)).astype(jnp.bfloat16)
    return (shared, lax.map(fit_subject, scans))

def reference(scans, start_maps):
    first_resp, first_maps = update(start_maps, scans)
    shared_resp, subject_maps = update(first_maps, scans)
    return (shared_resp, subject_maps)
```

```python
import functools
import math

import jax
import jax.numpy as jnp
from jax import lax
from jax.experimental import pallas as pl
from jax.experimental.pallas import tpu as pltpu
from jax.sharding import PartitionSpec as P

ITERS = 6
HALF = 64
LANES = 128
BF16 = jnp.bfloat16
F32 = jnp.float32
VMEM_LIMIT = 48 * 1024 * 1024
PARAMS = pltpu.CompilerParams(vmem_limit_bytes=VMEM_LIMIT)


def dot(a, b, contract=(1, 0), precision=None):
    return lax.dot_general(
        a,
        b,
        (((contract[0],), (contract[1],)), ((), ())),
        preferred_element_type=F32,
        precision=precision,
    )


def full_dot(a, b):
    return dot(a, b, precision=lax.Precision.HIGHEST)


def grid_rows_cols(n):
    rows = lax.broadcasted_iota(jnp.int32, (n, n), 0)
    cols = lax.broadcasted_iota(jnp.int32, (n, n), 1)
    return rows, cols


def pack_frames(by_frame):
    shares = by_frame.shape[0] // 32
    split = by_frame.reshape(shares, 2, 16, HALF)
    return jnp.concatenate([split[:, 0], split[:, 1]], axis=-1)


def unpack_frames(packed):
    shares = packed.shape[0]
    split = jnp.stack([packed[:, :, :HALF], packed[:, :, HALF:]], axis=1)
    return split.reshape(shares * 32, HALF)


def pack_grams(first, second):
    rows, cols = grid_rows_cols(HALF)
    joined = jnp.where(rows <= cols, first, second)
    wide = jnp.concatenate([joined[:32], joined[32:]], axis=1)
    diagonal = jnp.sum(jnp.where(rows == cols, second, 0.0), axis=0, keepdims=True)
    diagonal = jnp.concatenate([diagonal, diagonal], axis=1)
    return jnp.concatenate([wide, jnp.broadcast_to(diagonal, (16, LANES))], axis=0)


def unpack_grams(packed):
    rows, cols = grid_rows_cols(HALF)
    joined = jnp.concatenate([packed[:32, :HALF], packed[:32, HALF:]], axis=0)
    flipped = joined.T
    diagonal = packed[32:33, :HALF]
    first = jnp.where(rows <= cols, joined, flipped)
    second = jnp.where(rows > cols, joined, jnp.where(rows == cols, diagonal, flipped))
    return first, second


def polar_factors(first, second):
    rows, cols = grid_rows_cols(HALF)
    on_diagonal = rows == cols
    zero = jnp.zeros((HALF, HALF), F32)

    def trace(gram):
        return jnp.sum(jnp.where(on_diagonal, gram, 0.0), keepdims=True)

    squares = trace(first), trace(second)
    gram = jnp.concatenate(
        [
            jnp.concatenate([first / squares[0], zero], axis=1),
            jnp.concatenate([zero, second / squares[1]], axis=1),
        ],
        axis=0,
    )
    big_rows, big_cols = grid_rows_cols(LANES)
    identity = jnp.where(big_rows == big_cols, 1.0, 0.0)
    factor = None
    for step in range(ITERS):
        polar = 1.5 * identity - 0.5 * gram
        factor = polar if factor is None else full_dot(polar, factor)
        if step < ITERS - 1:
            gram = full_dot(full_dot(polar, gram), polar)
    scale = jnp.where(
        big_rows[:, :1] < HALF, lax.rsqrt(squares[0]), lax.rsqrt(squares[1])
    )
    return factor * scale


def start_kernel(maps_ref, scans_ref, out_ref, total):
    first = (pl.program_id(0) == 0) & (pl.program_id(1) == 0)
    last = (pl.program_id(0) == pl.num_programs(0) - 1) & (
        pl.program_id(1) == pl.num_programs(1) - 1
    )

    @pl.when(first)
    def _():
        total[...] = jnp.zeros_like(total)

    total[...] += dot(maps_ref[0], scans_ref[0])

    @pl.when(last)
    def _():
        out_ref[...] = pack_frames(total[...].T).astype(BF16)


def add_kernel(scale, parts_ref, out_ref):
    summed = jnp.sum(parts_ref[...].astype(F32), axis=0) * scale
    out_ref[...] = jnp.broadcast_to(summed[None], out_ref.shape)


def spread_kernel(parts_ref, out_ref):
    summed = jnp.sum(parts_ref[...], axis=0)
    out_ref[...] = jnp.broadcast_to(summed.astype(BF16)[None], out_ref.shape)


def spread_last_kernel(parts_ref, out_ref, resp_ref):
    summed = jnp.sum(parts_ref[...], axis=0)
    out_ref[...] = jnp.broadcast_to(summed.astype(BF16)[None], out_ref.shape)
    resp_ref[...] = unpack_frames(summed[None]).T


def load_shared(packed_ref, shared):
    shared[...] = unpack_frames(packed_ref[...]).T


def middle_kernel(packed_ref, scans_ref, out_ref, shared, gram, onward):
    subject, tile = pl.program_id(0), pl.program_id(1)
    last = tile == pl.num_programs(1) - 1

    @pl.when((subject == 0) & (tile == 0))
    def _():
        load_shared(packed_ref, shared)

    @pl.when(tile == 0)
    def _():
        gram[subject] = jnp.zeros_like(gram[subject])
        onward[subject] = jnp.zeros_like(onward[subject])

    scans = scans_ref[0]
    target = dot(shared[...], scans, (1, 1)).astype(BF16)
    gram[subject] += dot(target, target, (1, 1))
    onward[subject] += dot(target, scans)

    @pl.when(last & (subject == pl.num_programs(0) - 1))
    def _():
        by_frame = jnp.concatenate([onward[0].T, onward[1].T], axis=1)
        shares = out_ref.shape[0]
        out_ref[:, :32, :] = by_frame.reshape(shares, 32, LANES).astype(BF16)
        grams = pack_grams(gram[0], gram[1]).astype(BF16)
        out_ref[:, 32:, :] = jnp.broadcast_to(grams[None], (shares,) + grams.shape)


def polar_share_kernel(scale, parts_ref, out_ref):
    summed = jnp.sum(parts_ref[...].astype(F32), axis=0)
    factor = polar_factors(*unpack_grams(summed[32:]))
    stacked = jnp.concatenate([factor[:HALF, :HALF], factor[HALF:, HALF:]], axis=0)
    share = full_dot(summed[:32], stacked) * scale
    packed = pack_frames(share)
    out_ref[...] = jnp.broadcast_to(packed, out_ref.shape)


def target_kernel(packed_ref, scans_ref, target_ref, out_ref, shared, gram):
    subject, tile = pl.program_id(0), pl.program_id(1)
    last = tile == pl.num_programs(1) - 1

    @pl.when((subject == 0) & (tile == 0))
    def _():
        load_shared(packed_ref, shared)

    @pl.when(tile == 0)
    def _():
        gram[subject] = jnp.zeros_like(gram[subject])

    target = dot(shared[...], scans_ref[0], (1, 1)).astype(BF16)
    target_ref[0] = target
    gram[subject] += dot(target, target, (1, 1))

    @pl.when(last & (subject == pl.num_programs(0) - 1))
    def _():
        grams = pack_grams(gram[0], gram[1]).astype(BF16)
        out_ref[...] = jnp.broadcast_to(grams[None], out_ref.shape)


def maps_kernel(scale, parts_ref, target_ref, out_ref):
    summed = jnp.sum(parts_ref[...].astype(F32), axis=0)
    factor = polar_factors(*unpack_grams(summed)) * scale
    high = factor.astype(BF16)
    low = (factor - high.astype(F32)).astype(BF16)
    for subject in range(2):
        own = slice(subject * HALF, (subject + 1) * HALF)
        target = target_ref[subject]
        maps = dot(high[own, own], target) + dot(low[own, own], target)
        out_ref[subject] = maps.astype(BF16)


def whole(shape):
    return pl.BlockSpec(shape, lambda *_: (0,) * len(shape))


def small(body, out_shape, *args):
    return pl.pallas_call(body, out_shape=out_shape, compiler_params=PARAMS)(*args)


def shape_of(shape, dtype):
    return jax.ShapeDtypeStruct(shape, dtype)


def per_device(scans, start_maps):
    subj_dev, vox_dev, frames = scans.shape
    features = start_maps.shape[1]
    vox_ways, subj_ways = lax.axis_size("vox"), lax.axis_size("subj")
    voxels = vox_dev * vox_ways
    subjects = subj_dev * subj_ways
    norm_scale = 1.0 / (subjects * math.sqrt(voxels))
    tile = 1024
    grid = (subj_dev, vox_dev // tile)
    scans_spec = pl.BlockSpec((1, tile, frames), lambda i, t: (i, t, 0))
    share = (16, LANES)

    def across_vox(x):
        return lax.all_to_all(x, "vox", 0, 0)

    def across_subj(x):
        return lax.all_to_all(x, "subj", 0, 0)

    partial = pl.pallas_call(
        start_kernel,
        out_shape=shape_of((vox_ways,) + share, BF16),
        grid=grid,
        in_specs=[
            pl.BlockSpec((1, features, tile), lambda i, t: (i, 0, t)),
            scans_spec,
        ],
        out_specs=whole((vox_ways,) + share),
        scratch_shapes=[pltpu.VMEM((features, frames), F32)],
        compiler_params=PARAMS,
    )(start_maps, scans)
    parts = across_vox(partial)
    parts = across_subj(
        small(
            functools.partial(add_kernel, norm_scale),
            shape_of((subj_ways,) + share, F32),
            parts,
        )
    )
    shared = across_vox(
        small(spread_kernel, shape_of((vox_ways,) + share, BF16), parts)
    )

    rows = 32 + 48
    partial = pl.pallas_call(
        middle_kernel,
        out_shape=shape_of((vox_ways, rows, LANES), BF16),
        grid=grid,
        in_specs=[whole((vox_ways,) + share), scans_spec],
        out_specs=whole((vox_ways, rows, LANES)),
        scratch_shapes=[
            pltpu.VMEM((features, frames), BF16),
            pltpu.VMEM((subj_dev, features, features), F32),
            pltpu.VMEM((subj_dev, features, frames), F32),
        ],
        compiler_params=PARAMS,
    )(shared, scans)
    parts = across_vox(partial)
    parts = across_subj(
        small(
            functools.partial(polar_share_kernel, 1.0 / subjects),
            shape_of((subj_ways,) + share, F32),
            parts,
        )
    )
    shared, shared_resp = small(
        spread_last_kernel,
        [shape_of((vox_ways,) + share, BF16), shape_of((features, 32), F32)],
        parts,
    )
    shared = across_vox(shared)

    target, partial = pl.pallas_call(
        target_kernel,
        out_shape=[
            shape_of((subj_dev, features, vox_dev), BF16),
            shape_of((vox_ways, 48, LANES), BF16),
        ],
        grid=grid,
        in_specs=[whole((vox_ways,) + share), scans_spec],
        out_specs=[
            pl.BlockSpec((1, features, tile), lambda i, t: (i, 0, t)),
            whole((vox_ways, 48, LANES)),
        ],
        scratch_shapes=[
            pltpu.VMEM((features, frames), BF16),
            pltpu.VMEM((subj_dev, features, features), F32),
        ],
        compiler_params=PARAMS,
    )(shared, scans)
    parts = across_vox(partial)
    subject_maps = small(
        functools.partial(maps_kernel, math.sqrt(voxels)),
        shape_of((subj_dev, features, vox_dev), BF16),
        parts,
        target,
    )
    return (shared_resp, subject_maps)


def solution(mesh):
    placed = (P("subj", "vox", None), P("subj", None, "vox"))
    return jax.shard_map(
        per_device,
        mesh=mesh,
        in_specs=placed,
        out_specs=(P(None, "vox"), P("subj", None, "vox")),
        check_vma=False,
    )
```

```python
import functools
import math

import jax
import jax.numpy as jnp
from jax import lax
from jax.experimental import pallas as pl
from jax.experimental.pallas import tpu as pltpu
from jax.sharding import PartitionSpec as P

ITERS = 6
HALF = 64
LANES = 128
X_WAYS = 4
BF16 = jnp.bfloat16
F32 = jnp.float32
MIB = 1024 * 1024
PARAMS = pltpu.CompilerParams(vmem_limit_bytes=24 * MIB)
START_PARAMS = pltpu.CompilerParams(vmem_limit_bytes=42 * MIB)


def dot(a, b, contract=(1, 0), precision=None):
    return lax.dot_general(
        a,
        b,
        (((contract[0],), (contract[1],)), ((), ())),
        preferred_element_type=F32,
        precision=precision,
    )


def halves(x):
    high = x.astype(BF16)
    return high, (x - high.astype(F32)).astype(BF16)


def split_dot(a, b):
    a_high, a_low = halves(a)
    b_high, b_low = halves(b)
    left = jnp.concatenate([a_high, a_low], axis=1)
    right = jnp.concatenate(
        [
            jnp.concatenate([b_high, b_low], axis=1),
            jnp.concatenate([b_high, b_low], axis=1),
        ],
        axis=0,
    )
    both = dot(left, right)
    width = b.shape[1]
    return both[:, :width] + both[:, width:]


def grid_rows_cols(n):
    rows = lax.broadcasted_iota(jnp.int32, (n, n), 0)
    cols = lax.broadcasted_iota(jnp.int32, (n, n), 1)
    return rows, cols


def pack_frames(by_frame):
    shares = by_frame.shape[0] // 32
    split = by_frame.reshape(shares, 2, 16, HALF)
    return jnp.concatenate([split[:, 0], split[:, 1]], axis=-1)


def unpack_frames(packed):
    shares = packed.shape[0]
    split = jnp.stack([packed[:, :, :HALF], packed[:, :, HALF:]], axis=1)
    return split.reshape(shares * 32, HALF)


def pack_grams(first, second):
    rows, cols = grid_rows_cols(HALF)
    joined = jnp.where(rows <= cols, first, second)
    wide = jnp.concatenate([joined[:32], joined[32:]], axis=1)
    diagonal = jnp.sum(jnp.where(rows == cols, second, 0.0), axis=0, keepdims=True)
    diagonal = jnp.concatenate([diagonal, diagonal], axis=1)
    return jnp.concatenate([wide, jnp.broadcast_to(diagonal, (8, LANES))], axis=0)


def unpack_grams(packed):
    rows, cols = grid_rows_cols(HALF)
    joined = jnp.concatenate([packed[:32, :HALF], packed[:32, HALF:]], axis=0)
    flipped = joined.T
    diagonal = packed[32:33, :HALF]
    first = jnp.where(rows <= cols, joined, flipped)
    second = jnp.where(rows > cols, joined, jnp.where(rows == cols, diagonal, flipped))
    return first, second


def polar_factors(first, second):
    rows, cols = grid_rows_cols(HALF)
    on_diagonal = rows == cols
    zero = jnp.zeros((HALF, HALF), F32)

    def trace(gram):
        return jnp.sum(jnp.where(on_diagonal, gram, 0.0), keepdims=True)

    squares = trace(first), trace(second)
    gram = jnp.concatenate(
        [
            jnp.concatenate([first / squares[0], zero], axis=1),
            jnp.concatenate([zero, second / squares[1]], axis=1),
        ],
        axis=0,
    )
    big_rows, big_cols = grid_rows_cols(LANES)
    identity = jnp.where(big_rows == big_cols, 1.0, 0.0)
    factor = None
    for step in range(ITERS):
        polar = 1.5 * identity - 0.5 * gram
        factor = polar if factor is None else split_dot(polar, factor)
        if step < ITERS - 1:
            gram = split_dot(split_dot(polar, gram), polar)
    scale = jnp.where(
        big_rows[:, :1] < HALF, lax.rsqrt(squares[0]), lax.rsqrt(squares[1])
    )
    return factor * scale


def start_kernel(tile, maps_ref, scans_ref, out_ref, held, maps, maps_sem, sems):
    subjects, voxels, frames = held.shape
    maps_copy = pltpu.make_async_copy(maps_ref, maps, maps_sem)
    maps_copy.start()
    copies = []
    for subject in range(subjects):
        for begin in range(0, voxels, tile):
            part = (subject, slice(begin, begin + tile))
            copy = pltpu.make_async_copy(
                scans_ref.at[part], held.at[part], sems.at[len(copies)]
            )
            copy.start()
            copies.append((copy, part))
    maps_copy.wait()
    total = jnp.zeros((maps.shape[1], frames), F32)
    for copy, part in copies:
        copy.wait()
        total += dot(maps[part[0], :, part[1]], held[part])
    out_ref[...] = pack_frames(total.T).astype(BF16)


def add_kernel(scale, parts_ref, out_ref):
    summed = jnp.sum(parts_ref[...].astype(F32), axis=0) * scale
    out_ref[...] = jnp.broadcast_to(summed[None], out_ref.shape)


def spread_kernel(parts_ref, out_ref):
    summed = jnp.sum(parts_ref[...], axis=0)
    out_ref[...] = jnp.broadcast_to(summed.astype(BF16)[None], out_ref.shape)


def spread_last_kernel(parts_ref, out_ref, resp_ref):
    summed = jnp.sum(parts_ref[...], axis=0)
    out_ref[...] = jnp.broadcast_to(summed.astype(BF16)[None], out_ref.shape)
    resp_ref[...] = unpack_frames(summed[None]).T


def middle_kernel(packed_ref, scans_ref, out_ref):
    shared = unpack_frames(packed_ref[...]).T
    grams, onward = [], []
    for subject in range(2):
        scans = scans_ref[subject]
        target = dot(shared, scans, (1, 1)).astype(BF16)
        grams.append(dot(target, target, (1, 1)))
        onward.append(dot(target, scans).T)
    shares = out_ref.shape[0]
    by_frame = jnp.concatenate(onward, axis=1).reshape(shares, 32, LANES)
    packed = pack_grams(*grams)
    packed = jnp.broadcast_to(packed[None], (shares,) + packed.shape)
    out_ref[...] = jnp.concatenate([by_frame, packed], axis=1).astype(BF16)


def polar_share_kernel(scale, parts_ref, out_ref):
    summed = jnp.sum(parts_ref[...].astype(F32), axis=0)
    factor = polar_factors(*unpack_grams(summed[32:]))
    stacked = jnp.concatenate([factor[:HALF, :HALF], factor[HALF:, HALF:]], axis=0)
    high, low = halves(summed[:32])
    stack_high, stack_low = halves(stacked)
    share = dot(high, stack_high) + dot(low, stack_high) + dot(high, stack_low)
    share *= scale
    packed = pack_frames(share)
    out_ref[...] = jnp.broadcast_to(packed, out_ref.shape)


def target_kernel(packed_ref, scans_ref, target_ref, out_ref):
    shared = unpack_frames(packed_ref[...]).T
    grams = []
    for subject in range(2):
        target = dot(shared, scans_ref[subject], (1, 1)).astype(BF16)
        target_ref[subject] = target
        grams.append(dot(target, target, (1, 1)))
    packed = pack_grams(*grams).astype(BF16)
    out_ref[...] = jnp.broadcast_to(packed[None], out_ref.shape)


def maps_kernel(scale, parts_ref, target_ref, out_ref):
    summed = jnp.sum(parts_ref[...].astype(F32), axis=0)
    factor = polar_factors(*unpack_grams(summed)) * scale
    high = factor.astype(BF16)
    low = (factor - high.astype(F32)).astype(BF16)
    for subject in range(2):
        own = slice(subject * HALF, (subject + 1) * HALF)
        target = target_ref[subject]
        maps = dot(high[own, own], target) + dot(low[own, own], target)
        out_ref[subject] = maps.astype(BF16)


VMEM = pl.BlockSpec(memory_space=pltpu.VMEM)
HBM = pl.BlockSpec(memory_space=pltpu.HBM)


def shape_of(shape, dtype):
    return jax.ShapeDtypeStruct(shape, dtype)


def small(body, out_shape, *args):
    return pl.pallas_call(
        body,
        out_shape=out_shape,
        in_specs=[VMEM] * len(args),
        out_specs=jax.tree.map(lambda _: VMEM, out_shape),
        compiler_params=PARAMS,
    )(*args)


def start(maps, scans, shares, tile):
    subj_dev, features, vox_dev = maps.shape
    return pl.pallas_call(
        functools.partial(start_kernel, tile),
        out_shape=[
            shape_of((shares, 16, LANES), BF16),
            shape_of(scans.shape, scans.dtype),
        ],
        in_specs=[HBM, HBM],
        out_specs=[VMEM, VMEM],
        scratch_shapes=[
            pltpu.VMEM(maps.shape, maps.dtype),
            pltpu.SemaphoreType.DMA,
            pltpu.SemaphoreType.DMA((subj_dev * (vox_dev // tile),)),
        ],
        compiler_params=START_PARAMS,
    )(maps, scans)


def per_device(scans, start_maps):
    subj_dev, vox_dev, frames = scans.shape
    features = start_maps.shape[1]
    vox_ways, subj_ways = lax.axis_size("vox"), lax.axis_size("subj")
    voxels = vox_dev * vox_ways
    subjects = subj_dev * subj_ways
    norm_scale = 1.0 / (subjects * math.sqrt(voxels))
    share = (16, LANES)
    z_ways = vox_ways // X_WAYS
    same_x = [[z * X_WAYS + x for z in range(z_ways)] for x in range(X_WAYS)]
    same_z = [
        [s * vox_ways + z * X_WAYS + x for s in range(subj_ways) for x in range(X_WAYS)]
        for z in range(z_ways)
    ]

    def across_vox(x):
        return lax.all_to_all(x, "vox", 0, 0)

    def across_subj(x):
        return lax.all_to_all(x, "subj", 0, 0)

    def across_z(x):
        return lax.all_to_all(x, "vox", 0, 0, axis_index_groups=same_x)

    def across_subj_x(x):
        return lax.all_to_all(x, ("subj", "vox"), 0, 0, axis_index_groups=same_z)

    shares = subj_ways * X_WAYS
    partial, scans = start(start_maps, scans, shares, 512)
    parts = across_subj_x(partial)
    summed = functools.partial(add_kernel, norm_scale)
    parts = across_z(small(summed, shape_of((z_ways,) + share, F32), parts))
    shared = small(spread_kernel, shape_of((shares,) + share, BF16), parts)
    shared = across_subj_x(shared)

    partial = small(
        middle_kernel, shape_of((vox_ways, 72, LANES), BF16), shared, scans
    )
    parts = across_vox(partial)
    share_sum = functools.partial(polar_share_kernel, 1.0 / subjects)
    parts = across_subj(small(share_sum, shape_of((subj_ways,) + share, F32), parts))
    shared, shared_resp = small(
        spread_last_kernel,
        [shape_of((vox_ways,) + share, BF16), shape_of((features, 32), F32)],
        parts,
    )
    shared = across_vox(shared)

    target, partial = small(
        target_kernel,
        [
            shape_of((subj_dev, features, vox_dev), BF16),
            shape_of((vox_ways, 40, LANES), BF16),
        ],
        shared,
        scans,
    )
    parts = across_vox(partial)
    subject_maps = small(
        functools.partial(maps_kernel, math.sqrt(voxels)),
        shape_of((subj_dev, features, vox_dev), BF16),
        parts,
        target,
    )
    return (shared_resp, subject_maps)


def solution(mesh):
    placed = (P("subj", "vox", None), P("subj", None, "vox"))
    return jax.shard_map(
        per_device,
        mesh=mesh,
        in_specs=placed,
        out_specs=(P(None, "vox"), P("subj", None, "vox")),
        check_vma=False,
    )
```

```python
import functools
import math

import jax
import jax.numpy as jnp
from jax import lax
from jax.experimental import pallas as pl
from jax.experimental.pallas import tpu as pltpu
from jax.sharding import PartitionSpec as P

ITERS = 6
HALF = 64
LANES = 128
X_WAYS = 4
BF16 = jnp.bfloat16
F32 = jnp.float32
MIB = 1024 * 1024


def vmem(mib):
    return pltpu.CompilerParams(vmem_limit_bytes=int(mib * MIB))


def dot(a, b, contract=(1, 0), precision=None):
    return lax.dot_general(
        a,
        b,
        (((contract[0],), (contract[1],)), ((), ())),
        preferred_element_type=F32,
        precision=precision,
    )


def halves(x):
    high = x.astype(BF16)
    return high, (x - high.astype(F32)).astype(BF16)


def side_by_side(x):
    return jnp.concatenate(halves(x), axis=1)


def block_diagonal(x):
    lanes = lax.broadcasted_iota(jnp.int32, x.shape, 1)
    return jnp.concatenate(
        [jnp.where(lanes < HALF, x, 0.0), jnp.where(lanes < HALF, 0.0, x)], axis=0
    )


def split_operand(x):
    wide = side_by_side(block_diagonal(x))
    return jnp.concatenate([wide, wide], axis=0)


def split_dot(left, right):
    both = dot(side_by_side(left), right)
    return both[:, :LANES] + both[:, LANES:]


def grid_rows_cols(n):
    rows = lax.broadcasted_iota(jnp.int32, (n, n), 0)
    cols = lax.broadcasted_iota(jnp.int32, (n, n), 1)
    return rows, cols


def pack_frames(by_frame):
    shares = by_frame.shape[0] // 32
    split = by_frame.reshape(shares, 2, 16, HALF)
    return jnp.concatenate([split[:, 0], split[:, 1]], axis=-1)


def unpack_frames(packed):
    shares = packed.shape[0]
    split = jnp.stack([packed[:, :, :HALF], packed[:, :, HALF:]], axis=1)
    return split.reshape(shares * 32, HALF)


def pack_grams(first, second):
    rows, cols = grid_rows_cols(HALF)
    joined = jnp.where(rows <= cols, first, second)
    wide = jnp.concatenate([joined[:32], joined[32:]], axis=1)
    diagonal = jnp.sum(jnp.where(rows == cols, second, 0.0), axis=0, keepdims=True)
    diagonal = jnp.concatenate([diagonal, diagonal], axis=1)
    return jnp.concatenate([wide, jnp.broadcast_to(diagonal, (8, LANES))], axis=0)


def unpack_grams(packed):
    rows, cols = grid_rows_cols(HALF)
    joined = jnp.concatenate([packed[:32, :HALF], packed[:32, HALF:]], axis=0)
    flipped = joined.T
    diagonal = packed[32:33, :HALF]
    first = jnp.where(rows <= cols, joined, flipped)
    second = jnp.where(rows > cols, joined, jnp.where(rows == cols, diagonal, flipped))
    return first, second


def polar_factors(first, second):
    rows, cols = grid_rows_cols(HALF)

    def trace(gram):
        return jnp.sum(jnp.where(rows == cols, gram, 0.0), keepdims=True)

    wide_rows = lax.broadcasted_iota(jnp.int32, (HALF, LANES), 0)
    lanes = lax.broadcasted_iota(jnp.int32, (HALF, LANES), 1)
    identity = jnp.where(wide_rows == lanes % HALF, 1.0, 0.0)
    squares = jnp.where(lanes[:1] < HALF, trace(first), trace(second))
    gram = jnp.concatenate([first, second], axis=1) / squares
    factor = polar = 1.5 * identity - 0.5 * gram
    for step in range(1, ITERS):
        half_way = split_dot(polar, split_operand(gram))
        right = split_operand(polar)
        if step == 1:
            gram = split_dot(half_way, right)
        else:
            both = split_dot(jnp.concatenate([half_way, factor], axis=0), right)
            gram, factor = both[:HALF], both[HALF:]
        polar = 1.5 * identity - 0.5 * gram
    factor = split_dot(factor, split_operand(polar))
    return factor * lax.rsqrt(squares)


def start_kernel(tile, maps_ref, scans_ref, out_ref, held, maps, maps_sem, sems):
    subjects, voxels, frames = held.shape
    maps_copy = pltpu.make_async_copy(maps_ref, maps, maps_sem)
    maps_copy.start()
    copies = []
    for subject in range(subjects):
        for begin in range(0, voxels, tile):
            part = (subject, slice(begin, begin + tile))
            copy = pltpu.make_async_copy(
                scans_ref.at[part], held.at[part], sems.at[len(copies)]
            )
            copy.start()
            copies.append((copy, part))
    maps_copy.wait()
    total = jnp.zeros((maps.shape[1], frames), F32)
    for copy, part in copies:
        copy.wait()
        total += dot(maps[part[0], :, part[1]], held[part])
    out_ref[...] = pack_frames(total.T).astype(BF16)


def add_kernel(scale, parts_ref, out_ref):
    summed = jnp.sum(parts_ref[...].astype(F32), axis=0) * scale
    out_ref[...] = jnp.broadcast_to(summed[None], out_ref.shape)


def spread_kernel(parts_ref, out_ref):
    summed = jnp.sum(parts_ref[...], axis=0)
    out_ref[...] = jnp.broadcast_to(summed.astype(BF16)[None], out_ref.shape)


def spread_last_kernel(parts_ref, out_ref, resp_ref):
    summed = jnp.sum(parts_ref[...], axis=0)
    out_ref[...] = jnp.broadcast_to(summed.astype(BF16)[None], out_ref.shape)
    resp_ref[...] = summed


def targets_of(packed_ref, scans_ref):
    shared = unpack_frames(packed_ref[...]).T
    target = jnp.concatenate(
        [dot(shared, scans_ref[subject], (1, 1)).astype(BF16) for subject in range(2)],
        axis=0,
    )
    gram = dot(target, target, (1, 1))
    return target, pack_grams(gram[:HALF, :HALF], gram[HALF:, HALF:])


def middle_kernel(packed_ref, scans_ref, out_ref):
    target, packed = targets_of(packed_ref, scans_ref)
    onward = [dot(target[:HALF], scans_ref[0]), dot(target[HALF:], scans_ref[1])]
    shares = out_ref.shape[0]
    by_frame = jnp.concatenate(onward, axis=0).T.reshape(shares, 32, LANES)
    packed = jnp.broadcast_to(packed[None], (shares,) + packed.shape)
    out_ref[...] = jnp.concatenate([by_frame, packed], axis=1).astype(BF16)


def polar_share_kernel(scale, parts_ref, out_ref):
    summed = jnp.sum(parts_ref[...].astype(F32), axis=0)
    factor = polar_factors(*unpack_grams(summed[32:])) * scale
    share = split_dot(summed[:32], split_operand(factor))
    share = share[:, :HALF] + share[:, HALF:]
    out_ref[...] = jnp.broadcast_to(pack_frames(share), out_ref.shape)


def target_kernel(packed_ref, scans_ref, target_ref, out_ref):
    target, packed = targets_of(packed_ref, scans_ref)
    target_ref[...] = target
    out_ref[...] = jnp.broadcast_to(packed.astype(BF16)[None], out_ref.shape)


def maps_kernel(
    scale, pieces, parts_ref, target_ref, share_ref, out_ref, resp_ref, maps, resp, sems
):
    resp[...] = unpack_frames(share_ref[...][None])
    copies = [pltpu.make_async_copy(resp, resp_ref, sems.at[pieces])]
    copies[0].start()
    summed = jnp.sum(parts_ref[...].astype(F32), axis=0)
    factor = polar_factors(*unpack_grams(summed)) * scale
    left = side_by_side(block_diagonal(factor))
    target = target_ref[...]
    width = target.shape[1] // pieces
    for piece in range(pieces):
        part = slice(piece * width, (piece + 1) * width)
        right = jnp.concatenate([target[:, part], target[:, part]], axis=0)
        made = dot(left, right).astype(BF16)
        maps[:, :, part] = made.reshape(maps.shape[:2] + (width,))
        copies.append(
            pltpu.make_async_copy(
                maps.at[:, :, part], out_ref.at[:, :, part], sems.at[piece]
            )
        )
        copies[-1].start()
    for copy in copies:
        copy.wait()


VMEM = pl.BlockSpec(memory_space=pltpu.VMEM)
HBM = pl.BlockSpec(memory_space=pltpu.HBM)


def shape_of(shape, dtype):
    return jax.ShapeDtypeStruct(shape, dtype)


def call(body, mib, out_shape, args, arg_specs, out_specs, scratch=()):
    return pl.pallas_call(
        body,
        out_shape=out_shape,
        in_specs=arg_specs,
        out_specs=out_specs,
        scratch_shapes=scratch,
        compiler_params=vmem(mib),
    )(*args)


def small(body, out_shape, *args):
    out_specs = jax.tree.map(lambda _: VMEM, out_shape)
    return call(body, 24, out_shape, args, [VMEM] * len(args), out_specs)


def copies_of(count):
    return pltpu.SemaphoreType.DMA((count,))


def start(maps, scans, shares, tile):
    subj_dev, features, vox_dev = maps.shape
    return pl.pallas_call(
        functools.partial(start_kernel, tile),
        out_shape=[
            shape_of((shares, 16, LANES), BF16),
            shape_of(scans.shape, scans.dtype),
        ],
        in_specs=[HBM, HBM],
        out_specs=[VMEM, VMEM],
        scratch_shapes=[
            pltpu.VMEM(maps.shape, maps.dtype),
            pltpu.SemaphoreType.DMA,
            copies_of(subj_dev * (vox_dev // tile)),
        ],
        compiler_params=vmem(42),
    )(maps, scans)


def per_device(scans, start_maps):
    subj_dev, vox_dev, frames = scans.shape
    features = start_maps.shape[1]
    vox_ways, subj_ways = lax.axis_size("vox"), lax.axis_size("subj")
    voxels = vox_dev * vox_ways
    subjects = subj_dev * subj_ways
    norm_scale = 1.0 / (subjects * math.sqrt(voxels))
    share = (16, LANES)
    z_ways = vox_ways // X_WAYS
    same_x = [[z * X_WAYS + x for z in range(z_ways)] for x in range(X_WAYS)]
    same_z = [
        [s * vox_ways + z * X_WAYS + x for s in range(subj_ways) for x in range(X_WAYS)]
        for z in range(z_ways)
    ]

    def across_vox(x):
        return lax.all_to_all(x, "vox", 0, 0)

    def across_subj(x):
        return lax.all_to_all(x, "subj", 0, 0)

    def across_z(x):
        return lax.all_to_all(x, "vox", 0, 0, axis_index_groups=same_x)

    def across_subj_x(x):
        return lax.all_to_all(x, ("subj", "vox"), 0, 0, axis_index_groups=same_z)

    shares = subj_ways * X_WAYS
    partial, scans = start(start_maps, scans, shares, 512)
    parts = across_subj_x(partial)
    summed = functools.partial(add_kernel, norm_scale)
    parts = across_z(small(summed, shape_of((z_ways,) + share, F32), parts))
    shared = small(spread_kernel, shape_of((shares,) + share, BF16), parts)
    shared = across_subj_x(shared)

    gathered = shape_of((vox_ways, 72, LANES), BF16)
    parts = across_vox(small(middle_kernel, gathered, shared, scans))
    share_sum = functools.partial(polar_share_kernel, 1.0 / subjects)
    parts = across_subj(small(share_sum, shape_of((subj_ways,) + share, F32), parts))
    shared, own_share = small(
        spread_last_kernel,
        [shape_of((vox_ways,) + share, BF16), shape_of(share, F32)],
        parts,
    )
    shared = across_vox(shared)

    target_shapes = [
        shape_of((subj_dev * features, vox_dev), BF16),
        shape_of((vox_ways, 40, LANES), BF16),
    ]
    target, partial = small(target_kernel, target_shapes, shared, scans)
    parts = across_vox(partial)
    maps_shape = (subj_dev, features, vox_dev)
    pieces = 4
    subject_maps, shared_resp = call(
        functools.partial(maps_kernel, math.sqrt(voxels), pieces),
        20,
        [shape_of(maps_shape, BF16), shape_of((32, features), F32)],
        (parts, target, own_share),
        [VMEM] * 3,
        [HBM] * 2,
        [
            pltpu.VMEM(maps_shape, BF16),
            pltpu.VMEM((32, features), F32),
            copies_of(pieces + 1),
        ],
    )
    return (shared_resp.T, subject_maps)


def solution(mesh):
    placed = (P("subj", "vox", None), P("subj", None, "vox"))
    return jax.shard_map(
        per_device,
        mesh=mesh,
        in_specs=placed,
        out_specs=(P(None, "vox"), P("subj", None, "vox")),
        check_vma=False,
    )
```

```python
import functools
import math

import jax
import jax.numpy as jnp
from jax import lax
from jax.experimental import pallas as pl
from jax.experimental.pallas import tpu as pltpu
from jax.sharding import PartitionSpec as P

ITERS = 6
HALF = 64
LANES = 128
X_WAYS = 4
BF16 = jnp.bfloat16
F32 = jnp.float32
MIB = 1024 * 1024


def vmem(mib):
    return pltpu.CompilerParams(vmem_limit_bytes=int(mib * MIB))


def dot(a, b, contract=(1, 0), precision=None):
    return lax.dot_general(
        a,
        b,
        (((contract[0],), (contract[1],)), ((), ())),
        preferred_element_type=F32,
        precision=precision,
    )


def halves(x):
    high = x.astype(BF16)
    return high, (x - high.astype(F32)).astype(BF16)


def side_by_side(x):
    return jnp.concatenate(halves(x), axis=1)


def block_diagonal(x):
    lanes = lax.broadcasted_iota(jnp.int32, x.shape, 1)
    return jnp.concatenate(
        [jnp.where(lanes < HALF, x, 0.0), jnp.where(lanes < HALF, 0.0, x)], axis=0
    )


def split_operand(x):
    wide = side_by_side(block_diagonal(x))
    return jnp.concatenate([wide, wide], axis=0)


def split_dot(left, right):
    both = dot(side_by_side(left), right)
    return both[:, :LANES] + both[:, LANES:]


def grid_rows_cols(n):
    rows = lax.broadcasted_iota(jnp.int32, (n, n), 0)
    cols = lax.broadcasted_iota(jnp.int32, (n, n), 1)
    return rows, cols


def pack_frames(by_frame):
    shares = by_frame.shape[0] // 32
    split = by_frame.reshape(shares, 2, 16, HALF)
    return jnp.concatenate([split[:, 0], split[:, 1]], axis=-1)


def unpack_frames(packed):
    shares = packed.shape[0]
    split = jnp.stack([packed[:, :, :HALF], packed[:, :, HALF:]], axis=1)
    return split.reshape(shares * 32, HALF)


def pack_grams(first, second):
    rows, cols = grid_rows_cols(HALF)
    joined = jnp.where(rows <= cols, first, second)
    wide = jnp.concatenate([joined[:32], joined[32:]], axis=1)
    diagonal = jnp.sum(jnp.where(rows == cols, second, 0.0), axis=0, keepdims=True)
    diagonal = jnp.concatenate([diagonal, diagonal], axis=1)
    return jnp.concatenate([wide, jnp.broadcast_to(diagonal, (8, LANES))], axis=0)


def unpack_grams(packed):
    rows, cols = grid_rows_cols(HALF)
    joined = jnp.concatenate([packed[:32, :HALF], packed[:32, HALF:]], axis=0)
    flipped = joined.T
    diagonal = packed[32:33, :HALF]
    first = jnp.where(rows <= cols, joined, flipped)
    second = jnp.where(rows > cols, joined, jnp.where(rows == cols, diagonal, flipped))
    return first, second


def polar_factors(first, second):
    rows, cols = grid_rows_cols(HALF)

    def trace(gram):
        return jnp.sum(jnp.where(rows == cols, gram, 0.0), keepdims=True)

    wide_rows = lax.broadcasted_iota(jnp.int32, (HALF, LANES), 0)
    lanes = lax.broadcasted_iota(jnp.int32, (HALF, LANES), 1)
    identity = jnp.where(wide_rows == lanes % HALF, 1.0, 0.0)
    squares = jnp.where(lanes[:1] < HALF, trace(first), trace(second))
    gram = jnp.concatenate([first, second], axis=1) / squares
    factor = polar = 1.5 * identity - 0.5 * gram
    for step in range(1, ITERS):
        half_way = split_dot(polar, split_operand(gram))
        right = split_operand(polar)
        if step == 1:
            gram = split_dot(half_way, right)
        else:
            both = split_dot(jnp.concatenate([half_way, factor], axis=0), right)
            gram, factor = both[:HALF], both[HALF:]
        polar = 1.5 * identity - 0.5 * gram
    factor = split_dot(factor, split_operand(polar))
    return factor * lax.rsqrt(squares)


def start_kernel(tile, maps_ref, scans_ref, out_ref, held, maps, maps_sem, sems):
    subjects, voxels, frames = held.shape
    maps_copy = pltpu.make_async_copy(maps_ref, maps, maps_sem)
    maps_copy.start()
    copies = []
    for subject in range(subjects):
        for begin in range(0, voxels, tile):
            part = (subject, slice(begin, begin + tile))
            copy = pltpu.make_async_copy(
                scans_ref.at[part], held.at[part], sems.at[len(copies)]
            )
            copy.start()
            copies.append((copy, part))
    maps_copy.wait()
    total = jnp.zeros((maps.shape[1], frames), F32)
    for copy, part in copies:
        copy.wait()
        total += dot(maps[part[0], :, part[1]], held[part])
    out_ref[...] = pack_frames(total.T).astype(BF16)


def add_kernel(scale, parts_ref, out_ref):
    summed = jnp.sum(parts_ref[...].astype(F32), axis=0) * scale
    out_ref[...] = jnp.broadcast_to(summed.astype(BF16)[None], out_ref.shape)


def spread_kernel(parts_ref, out_ref):
    summed = jnp.sum(parts_ref[...].astype(F32), axis=0)
    out_ref[...] = jnp.broadcast_to(summed.astype(BF16)[None], out_ref.shape)


def spread_last_kernel(parts_ref, out_ref, resp_ref):
    summed = jnp.sum(parts_ref[...].astype(F32), axis=0)
    out_ref[...] = jnp.broadcast_to(summed.astype(BF16)[None], out_ref.shape)
    resp_ref[...] = summed


def targets_of(packed_ref, scans_ref):
    shared = unpack_frames(packed_ref[...]).T
    target = jnp.concatenate(
        [dot(shared, scans_ref[subject], (1, 1)).astype(BF16) for subject in range(2)],
        axis=0,
    )
    gram = dot(target, target, (1, 1))
    return target, pack_grams(gram[:HALF, :HALF], gram[HALF:, HALF:])


def middle_kernel(packed_ref, scans_ref, out_ref):
    target, packed = targets_of(packed_ref, scans_ref)
    onward = [dot(target[:HALF], scans_ref[0]), dot(target[HALF:], scans_ref[1])]
    by_frame = jnp.concatenate(onward, axis=0).T.astype(BF16)
    packed = packed.astype(BF16)
    ways = out_ref.shape[0]
    shares = by_frame.shape[0] // 32
    for x in range(ways):
        own = [by_frame[v * 32 : (v + 1) * 32] for v in range(x, shares, ways)]
        out_ref[x] = jnp.concatenate(own + [packed], axis=0)


def regroup_kernel(parts_ref, out_ref):
    summed = jnp.sum(parts_ref[...].astype(F32), axis=0).astype(BF16)
    ways = out_ref.shape[0]
    packed = summed[ways * 32 :]
    for z in range(ways):
        out_ref[z] = jnp.concatenate([summed[z * 32 : (z + 1) * 32], packed], axis=0)


def polar_share_kernel(scale, parts_ref, out_ref):
    summed = jnp.sum(parts_ref[...].astype(F32), axis=0)
    factor = polar_factors(*unpack_grams(summed[32:])) * scale
    share = split_dot(summed[:32], split_operand(factor))
    share = share[:, :HALF] + share[:, HALF:]
    packed = pack_frames(share).astype(BF16)
    out_ref[...] = jnp.broadcast_to(packed, out_ref.shape)


def target_kernel(packed_ref, scans_ref, target_ref, out_ref):
    target, packed = targets_of(packed_ref, scans_ref)
    target_ref[...] = target
    out_ref[...] = jnp.broadcast_to(packed.astype(BF16)[None], out_ref.shape)


def maps_kernel(
    scale, pieces, parts_ref, target_ref, share_ref, out_ref, resp_ref, maps, resp, sems
):
    resp[...] = unpack_frames(share_ref[...][None])
    copies = [pltpu.make_async_copy(resp, resp_ref, sems.at[pieces])]
    copies[0].start()
    summed = jnp.sum(parts_ref[...].astype(F32), axis=0)
    factor = polar_factors(*unpack_grams(summed)) * scale
    left = side_by_side(block_diagonal(factor))
    target = target_ref[...]
    width = target.shape[1] // pieces
    for piece in range(pieces):
        part = slice(piece * width, (piece + 1) * width)
        right = jnp.concatenate([target[:, part], target[:, part]], axis=0)
        made = dot(left, right).astype(BF16)
        maps[:, :, part] = made.reshape(maps.shape[:2] + (width,))
        copies.append(
            pltpu.make_async_copy(
                maps.at[:, :, part], out_ref.at[:, :, part], sems.at[piece]
            )
        )
        copies[-1].start()
    for copy in copies:
        copy.wait()


VMEM = pl.BlockSpec(memory_space=pltpu.VMEM)
HBM = pl.BlockSpec(memory_space=pltpu.HBM)


def shape_of(shape, dtype):
    return jax.ShapeDtypeStruct(shape, dtype)


def call(body, mib, out_shape, args, arg_specs, out_specs, scratch=()):
    return pl.pallas_call(
        body,
        out_shape=out_shape,
        in_specs=arg_specs,
        out_specs=out_specs,
        scratch_shapes=scratch,
        compiler_params=vmem(mib),
    )(*args)


def small(body, out_shape, *args):
    out_specs = jax.tree.map(lambda _: VMEM, out_shape)
    return call(body, 24, out_shape, args, [VMEM] * len(args), out_specs)


def copies_of(count):
    return pltpu.SemaphoreType.DMA((count,))


def start(maps, scans, shares, tile):
    subj_dev, features, vox_dev = maps.shape
    return pl.pallas_call(
        functools.partial(start_kernel, tile),
        out_shape=[
            shape_of((shares, 16, LANES), BF16),
            shape_of(scans.shape, scans.dtype),
        ],
        in_specs=[HBM, HBM],
        out_specs=[VMEM, VMEM],
        scratch_shapes=[
            pltpu.VMEM(maps.shape, maps.dtype),
            pltpu.SemaphoreType.DMA,
            copies_of(subj_dev * (vox_dev // tile)),
        ],
        compiler_params=vmem(42),
    )(maps, scans)


def per_device(scans, start_maps):
    subj_dev, vox_dev, frames = scans.shape
    features = start_maps.shape[1]
    vox_ways, subj_ways = lax.axis_size("vox"), lax.axis_size("subj")
    voxels = vox_dev * vox_ways
    subjects = subj_dev * subj_ways
    norm_scale = 1.0 / (subjects * math.sqrt(voxels))
    share = (16, LANES)
    z_ways = vox_ways // X_WAYS
    same_x = [[z * X_WAYS + x for z in range(z_ways)] for x in range(X_WAYS)]
    own_z = [[z * X_WAYS + x for x in range(X_WAYS)] for z in range(z_ways)]
    same_z = [
        [s * vox_ways + z * X_WAYS + x for s in range(subj_ways) for x in range(X_WAYS)]
        for z in range(z_ways)
    ]

    def across_vox(x):
        return lax.all_to_all(x, "vox", 0, 0)

    def across_subj(x):
        return lax.all_to_all(x, "subj", 0, 0)

    def across_z(x):
        return lax.all_to_all(x, "vox", 0, 0, axis_index_groups=same_x)

    def across_x(x):
        return lax.all_to_all(x, "vox", 0, 0, axis_index_groups=own_z)

    def across_subj_x(x):
        return lax.all_to_all(x, ("subj", "vox"), 0, 0, axis_index_groups=same_z)

    shares = subj_ways * X_WAYS
    partial, scans = start(start_maps, scans, shares, 512)
    parts = across_subj_x(partial)
    summed = functools.partial(add_kernel, norm_scale)
    parts = across_z(small(summed, shape_of((z_ways,) + share, BF16), parts))
    shared = small(spread_kernel, shape_of((shares,) + share, BF16), parts)
    shared = across_subj_x(shared)

    by_x = shape_of((X_WAYS, z_ways * 32 + 40, LANES), BF16)
    parts = across_x(small(middle_kernel, by_x, shared, scans))
    by_z = shape_of((z_ways, 72, LANES), BF16)
    parts = across_z(small(regroup_kernel, by_z, parts))
    share_sum = functools.partial(polar_share_kernel, 1.0 / subjects)
    parts = across_subj(small(share_sum, shape_of((subj_ways,) + share, BF16), parts))
    shared, own_share = small(
        spread_last_kernel,
        [shape_of((vox_ways,) + share, BF16), shape_of(share, F32)],
        parts,
    )
    shared = across_vox(shared)

    target_shapes = [
        shape_of((subj_dev * features, vox_dev), BF16),
        shape_of((vox_ways, 40, LANES), BF16),
    ]
    target, partial = small(target_kernel, target_shapes, shared, scans)
    parts = across_vox(partial)
    maps_shape = (subj_dev, features, vox_dev)
    pieces = 4
    subject_maps, shared_resp = call(
        functools.partial(maps_kernel, math.sqrt(voxels), pieces),
        20,
        [shape_of(maps_shape, BF16), shape_of((32, features), F32)],
        (parts, target, own_share),
        [VMEM] * 3,
        [HBM] * 2,
        [
            pltpu.VMEM(maps_shape, BF16),
            pltpu.VMEM((32, features), F32),
            copies_of(pieces + 1),
        ],
    )
    return (shared_resp.T, subject_maps)


def solution(mesh):
    placed = (P("subj", "vox", None), P("subj", None, "vox"))
    return jax.shard_map(
        per_device,
        mesh=mesh,
        in_specs=placed,
        out_specs=(P(None, "vox"), P("subj", None, "vox")),
        check_vma=False,
    )
```
